1024 devices in a mesh: fsdp: 64 (over y, z_lo), tensor: 16 (over z_hi, x, core).
Axes of the slice: x: 4, y: 8, z: 16 (z_hi: 2, z_lo: 8; z = z_hi * 8 + z_lo), core: 2. Of those that a mesh axis runs over, the one named last changes fastest.
Arguments:
- tokens: bfloat16 [8192, 4096], P(('fsdp', 'tensor')), may hold values from -24 to 24
- weight: bfloat16 [4096, 14336], P('fsdp', 'tensor'), may hold values from -0.25 to 0.25
- tile_pick: int32 [32, 16], replicated, may hold values from -1 to 6
- cotangent: bfloat16 [8192, 14336], P('fsdp', 'tensor'), may hold values from -6 to 6
Outputs:
- activated: bfloat16 [8192, 14336], P('fsdp', 'tensor')
- token_grad: bfloat16 [8192, 4096], P(('fsdp', 'tensor'))
- weight_grad: float32 [4096, 14336], P('fsdp', 'tensor')
The draws below stay inside these ranges and needn't reach their ends.
Inputs may be any that keep to these rules, and one draw needn't show every extreme that they name: tile_pick[r, g] is the kept tile among the 7 tiles of column group g in tile row r, or -1 when none of them is kept.
All inputs are finite; a program needn't handle non-finite values.
Results may differ from the reference program's by a relative error of at most 0.013.
Values may be sent and summed in bfloat16 or wider, within the bound.
A program may use at most 32 MiB of HBM per device.

```python
import math
import jax
import jax.numpy as jnp
from jax import lax

D = 4096
F = 14336
TILE = 128
GROUP = 7
TOKENS = 8192
TILE_ROWS = 32
GROUPS = 16
N_TENSOR = 16


def plant(array, rng, low, largest):
    extent = array.shape
    place = [jax.random.randint(jax.random.fold_in(rng, axis), (), 0, extent[axis]) for axis in range(len(extent))]
    array = array.at[tuple(place)].set(low)
    longest = extent.index(max(extent))
    place[longest] = (place[longest] + 1) % extent[longest]
    return array.at[tuple(place)].set(largest)


def raised(result, stream_key, source, target, shards_of, factor):
    owner, partner = [(jnp.arange(result.shape[dim]) // (result.shape[dim] // shards_of)).reshape([-1 if axis == dim else 1 for axis in range(result.ndim)]) for dim in (source, target)]
    chosen = jax.random.permutation(stream_key, shards_of)[partner]
    strong = (owner == chosen) | (owner == (partner + shards_of // 2) % shards_of)
    return jnp.where(strong, factor * result, result)


def level_of(stream_key, extent, shards, smallest, top_value):
    loudness = 1.0
    for position, shards_of in shards:
        draws = jax.random.uniform(jax.random.fold_in(jax.random.fold_in(stream_key, 6), position), (shards_of,), jnp.float32, smallest / len(shards), top_value / len(shards))
        loudness = loudness * jnp.repeat(jnp.exp(draws), extent[position] // shards_of).reshape((-1,) + (1,) * (len(extent) - 1 - position))
    return loudness


def centred(key, extent, width, reach, shards=(), held_as=jnp.bfloat16):
    level = level_of(key, extent, shards, -0.22, 0.18) if shards else 1.0
    values = jax.random.normal(key, extent, jnp.float32) * width * level
    return jnp.minimum(jnp.maximum(values, -reach), reach).astype(held_as)


def gaussian_with(rng, shape, width, bound, cuts, heavy, held_as=jnp.bfloat16):
    result = width * jax.random.normal(rng, shape, jnp.float32)
    if cuts:
        result = result * level_of(rng, shape, cuts, -0.22, 0.18)
    return jnp.clip(raised(result, jax.random.fold_in(rng, 3), *heavy), -bound, bound).astype(held_as)


def setup_inputs(seed: int = 0) -> dict:
    seeds = jax.random.split(jax.random.key(seed), 5)
    tokens = gaussian_with(seeds[0], (TOKENS, D), 1.0, 24.0, ((0, 1024),), (0, 1, 1024, 6.0))
    weight = centred(seeds[1], (D, F), (D // (GROUP + 1)) ** -0.5, 0.25, ((0, 64), (1, 16)))
    tile_pick = plant(jax.random.randint(seeds[2], (TILE_ROWS, GROUPS), -1, GROUP), jax.random.fold_in(seeds[2], 1), -1, GROUP - 1).astype(jnp.int32)
    cotangent = centred(seeds[3], (TOKENS, F), 1.0, 6.0, ((0, 64), (1, 16)))
    return {"tokens": tokens, "weight": weight, "tile_pick": tile_pick, "cotangent": cotangent}


precise_mode = lax.Precision.HIGHEST


def reference(tokens, weight, tile_pick, cotangent):
    tile_rows = D // TILE
    groups = F // (TILE * GROUP)
    slots = groups // N_TENSOR
    block_len = math.gcd(TOKENS, 512)
    blocks = TOKENS // block_len
    onehot = (tile_pick[:, :, None] == jnp.arange(GROUP, dtype=jnp.int32)[None, None, :]).astype(jnp.float32)
    weight_five = weight.astype(jnp.float32).reshape(tile_rows, TILE, groups, GROUP, TILE)
    packed = jnp.einsum('rkgjn,rgj->rkgn', weight_five, onehot, precision=precise_mode).astype(jnp.bfloat16)
    packed_f = packed.astype(jnp.float32)
    packed_split = packed_f.reshape(tile_rows, TILE, N_TENSOR, slots, TILE)

    def one_block(running, inputs):
        tok_block, cot_block = inputs
        tok_three = tok_block.astype(jnp.float32).reshape(block_len, tile_rows, TILE)
        partial_value = jnp.einsum('trk,rkgn->trgn', tok_three, packed_f, precision=precise_mode)
        pre_act = jnp.einsum('trgn,rgj->tgjn', partial_value, onehot, precision=precise_mode).reshape(block_len, F)
        sigmoid_pre = jax.nn.sigmoid(pre_act)
        activated = (pre_act * sigmoid_pre).astype(jnp.bfloat16)
        dpre = (cot_block.astype(jnp.float32) * sigmoid_pre * (1.0 + pre_act * (1.0 - sigmoid_pre))).astype(jnp.bfloat16)
        dpre_four = dpre.astype(jnp.float32).reshape(block_len, groups, GROUP, TILE)
        dpacked = jnp.einsum('tgjn,rgj->trgn', dpre_four, onehot, precision=precise_mode).astype(jnp.bfloat16)
        dpacked_f = dpacked.astype(jnp.float32)
        per_panel = jnp.einsum('trpsn,rkpsn->tprk', dpacked_f.reshape(block_len, tile_rows, N_TENSOR, slots, TILE), packed_split, precision=precise_mode)
        per_panel = lax.optimization_barrier(per_panel.astype(jnp.bfloat16)).astype(jnp.float32)
        token_grad = jnp.sum(per_panel, axis=1).reshape(block_len, D).astype(jnp.bfloat16)
        running = running + jnp.einsum('trk,trgn->rkgn', tok_three, dpacked_f, precision=precise_mode)
        return running, (activated, token_grad)

    start_sum = jnp.zeros((tile_rows, TILE, groups, TILE), jnp.float32)
    tok_blocks = tokens.reshape(blocks, block_len, D)
    cot_blocks = cotangent.reshape(blocks, block_len, F)
    tile_sums, (act_blocks, grad_blocks) = lax.scan(one_block, start_sum, (tok_blocks, cot_blocks))
    weight_grad = (tile_sums[:, :, :, None, :] * onehot[:, None, :, :, None]).reshape(D, F)
    return act_blocks.reshape(TOKENS, F), grad_blocks.reshape(TOKENS, D), weight_grad
```

```python
import functools

import jax
import jax.numpy as jnp
from jax import lax
from jax.experimental import pallas as pl
from jax.experimental.pallas import tpu as pltpu
from jax.sharding import PartitionSpec as P

TILE = 128
GROUP = 7
BF = jnp.bfloat16
F32 = jnp.float32


def kernel(dims, tok_in, w_in, picks, cot_in, act_out, tg_out, wg_out,
           tok, panel, xbuf, acc, dpre, dpick, pf, pb, g1, sb, g2, rb, g3,
           vf, vb, h1, uf, ub, h2,
           t1_s, t1_r, t2_s, t2_r, t3_s, t3_r, w1_s, w1_r, w2_s, w2_r,
           g1_s, g1_r, g2_s, g2_r, g3_s, g3_r, h1_s, h1_r, h2_s, h2_r):
    Y, Z, H, X = dims
    C = 2
    rows = w_in.shape[0]
    D = tok_in.shape[1]
    quarter = D // 4
    tile_rows = D // TILE
    f = lax.axis_index("fsdp")
    t = lax.axis_index("tensor")
    y, z = f // Z, f % Z
    h, x, c = t // (X * C), (t // C) % X, t % C

    def dev(yy=None, zz=None, hh=None, xx=None, cc=None):
        yy = y if yy is None else yy
        zz = z if zz is None else zz
        hh = h if hh is None else hh
        xx = x if xx is None else xx
        cc = c if cc is None else cc
        return (yy * Z + zz, (hh * X + xx) * C + cc)

    peers = (
        [dev(yy=(y + d) % Y) for d in range(1, Y)]
        + [dev(zz=(z + d) % Z) for d in range(1, Z)]
        + [dev(xx=(x + d) % X) for d in range(1, X)]
        + [dev(hh=1 - h), dev(cc=1 - c)]
    )
    barrier = pltpu.get_barrier_semaphore()
    for p in peers:
        pl.semaphore_signal(barrier, inc=1, device_id=p, device_id_type=pl.DeviceIdType.MESH)

    def copy(src, dst, ss, rs, device):
        return pltpu.make_async_remote_copy(
            src_ref=src, dst_ref=dst, send_sem=ss, recv_sem=rs,
            device_id=device, device_id_type=pl.DeviceIdType.MESH)

    def chosen(p, j):
        return jnp.full((1, TILE), (p == j).astype(F32)).astype(BF)

    def piece(cc, xx, hh):
        return (cc * X + xx) * H + hh

    own = tok_in[...].astype(F32)
    own = jnp.concatenate([own[:, k * quarter:(k + 1) * quarter] for k in range(4)], axis=0)
    me = piece(c, x, h)
    tok[me] = own.astype(BF)
    my_pick = picks[(f * rows) // TILE, t]
    mine = jnp.zeros((rows, TILE), BF)
    for j in range(GROUP):
        mine += w_in[:, j * TILE:(j + 1) * TILE] * chosen(my_pick, j)
    panel[f] = mine

    pl.semaphore_wait(barrier, len(peers))

    sent = []

    def go(src, dst, ss, rs, device):
        op = copy(src, dst, ss, rs, device)
        op.start()
        sent.append(op)

    def arrived(dst, ss, rs):
        copy(dst, dst, ss, rs, dev(cc=1 - c)).wait_recv()

    go(tok.at[me], tok.at[me], t1_s.at[0], t1_r.at[0], dev(hh=1 - h))
    for d in range(1, Z):
        go(panel.at[f], panel.at[f], w1_s.at[d], w1_r.at[d], dev(zz=(z + d) % Z))
    for d in range(1, X):
        go(tok.at[me], tok.at[me], t2_s.at[0, d], t2_r.at[0, d], dev(xx=(x + d) % X))
    go(tok.at[me], tok.at[me], t3_s.at[0, 0], t3_r.at[0, 0], dev(cc=1 - c))
    for d in range(1, Z):
        arrived(panel.at[y * Z + (z - d + Z) % Z], w1_s.at[d], w1_r.at[d])
    for d in range(1, Y):
        go(panel.at[pl.ds(y * Z, Z)], panel.at[pl.ds(y * Z, Z)], w2_s.at[d], w2_r.at[d],
           dev(yy=(y + d) % Y))
    for d in range(1, X):
        src = piece(c, (x - d + X) % X, h)
        arrived(tok.at[src], t2_s.at[0, d], t2_r.at[0, d])
        go(tok.at[src], tok.at[src], t3_s.at[0, d], t3_r.at[0, d], dev(cc=1 - c))
    src = piece(c, x, 1 - h)
    arrived(tok.at[src], t1_s.at[0], t1_r.at[0])
    for d in range(1, X):
        go(tok.at[src], tok.at[src], t2_s.at[1, d], t2_r.at[1, d], dev(xx=(x + d) % X))
    go(tok.at[src], tok.at[src], t3_s.at[1, 0], t3_r.at[1, 0], dev(cc=1 - c))
    for d in range(1, X):
        src = piece(c, (x - d + X) % X, 1 - h)
        arrived(tok.at[src], t2_s.at[1, d], t2_r.at[1, d])
        go(tok.at[src], tok.at[src], t3_s.at[1, d], t3_r.at[1, d], dev(cc=1 - c))
    for k in range(2):
        for d in range(X):
            src = piece(1 - c, (x - d + X) % X, h if k == 0 else 1 - h)
            arrived(tok.at[src], t3_s.at[k, d], t3_r.at[k, d])

    def assemble(i, _):
        hh, xx = i // X, i % X
        a = tok[piece(0, xx, hh)].astype(F32)
        b = tok[piece(1, xx, hh)].astype(F32)
        at = pl.ds(pl.multiple_of(i * 16, 16), 16)
        for k in range(4):
            both = jnp.concatenate([a[k * 8:k * 8 + 8], b[k * 8:k * 8 + 8]], axis=0)
            xbuf[at, k * quarter:(k + 1) * quarter] = both.astype(BF)
        return 0

    lax.fori_loop(0, H * X, assemble, 0)

    for d in range(1, Y):
        arrived(panel.at[pl.ds((y - d + Y) % Y * Z, Z)], w2_s.at[d], w2_r.at[d])

    blocks = TILE // rows
    acc[...] = jnp.zeros_like(acc)

    def tile_of(r):
        return panel[pl.ds(r * blocks, blocks)].reshape(TILE, TILE)

    def forward(i, _):
        r = i * 2
        p0, p1 = picks[r, t], picks[r + 1, t]
        w0, w1 = tile_of(r), tile_of(r + 1)
        cols = []
        for j in range(GROUP):
            cols.append(jnp.concatenate([w0 * chosen(p0, j), w1 * chosen(p1, j)], axis=0))
        wide = jnp.concatenate(cols, axis=1)
        acc[...] += jnp.dot(xbuf[:, pl.ds(pl.multiple_of(i * 2 * TILE, 2 * TILE), 2 * TILE)], wide,
                            preferred_element_type=F32)
        return 0

    lax.fori_loop(0, tile_rows // 2, forward, 0)
    for j in range(GROUP):
        at = slice(j * TILE, (j + 1) * TILE)
        pre = acc[:, at]
        s = jax.nn.sigmoid(pre)
        act_out[:, at] = (pre * s).astype(BF)
        dpre[:, at] = (cot_in[:, at].astype(F32) * s * (1.0 + pre * (1.0 - s))).astype(BF)

    def pick(r, _):
        p = picks[r, t]
        total = jnp.zeros((dpre.shape[0], TILE), BF)
        for j in range(GROUP):
            total += dpre[:, j * TILE:(j + 1) * TILE] * chosen(p, j)
        dpick[:, pl.ds(pl.multiple_of(r * TILE, TILE), TILE)] = total
        return 0

    lax.fori_loop(0, tile_rows, pick, 0)

    def weight_part(r, _):
        at = pl.ds(pl.multiple_of(r * TILE, TILE), TILE)
        g = lax.dot_general(xbuf[:, at], dpick[:, at], (((0,), (0,)), ((), ())),
                            preferred_element_type=F32)
        g = g.reshape(blocks, rows, TILE)
        vf[pl.ds(r * blocks, blocks)] = g
        vb[pl.ds(r * blocks, blocks)] = g.astype(BF)
        return 0

    lax.fori_loop(0, tile_rows, weight_part, 0)
    for d in range(1, Y):
        go(vb.at[pl.ds((y + d) % Y * Z, Z)], h1.at[d], h1_s.at[d], h1_r.at[d], dev(yy=(y + d) % Y))

    def token_part(r, _):
        at = pl.ds(pl.multiple_of(r * TILE, TILE), TILE)
        pf[:, at] = lax.dot_general(dpick[:, at], tile_of(r), (((1,), (1,)), ((), ())),
                                    preferred_element_type=F32)
        return 0

    lax.fori_loop(0, tile_rows, token_part, 0)

    def row_piece(cc, xx, hh):
        at = pl.ds(pl.multiple_of(((hh * X + xx) * C + cc) * 8, 8), 8)
        return jnp.concatenate(
            [pf[at, k * quarter:(k + 1) * quarter] for k in range(4)], axis=0)

    def to_sibling(i, _):
        pb[i] = row_piece(1 - c, i // H, i % H).astype(BF)
        return 0

    lax.fori_loop(0, X * H, to_sibling, 0)
    go(pb, g1, g1_s.at[0], g1_r.at[0], dev(cc=1 - c))
    arrived(g1, g1_s.at[0], g1_r.at[0])

    def chip_sum(i, _):
        sb[i] = (row_piece(c, i // H, i % H) + g1[i].astype(F32)).astype(BF)
        return 0

    lax.fori_loop(0, X * H, chip_sum, 0)
    for d in range(1, X):
        to = (x + d) % X
        go(sb.at[pl.ds(to * H, H)], g2.at[d], g2_s.at[d], g2_r.at[d], dev(xx=to))
    for d in range(1, X):
        arrived(g2.at[d], g2_s.at[d], g2_r.at[d])

    def line_sum(hh):
        total = row_piece(c, x, hh) + g1[x * H + hh].astype(F32)
        for d in range(1, X):
            total += g2[d, hh].astype(F32)
        return total

    rb[...] = line_sum(1 - h).astype(BF)
    go(rb, g3, g3_s.at[0], g3_r.at[0], dev(hh=1 - h))

    for d in range(1, Y):
        arrived(h1.at[d], h1_s.at[d], h1_r.at[d])

    def y_sum(i, _):
        total = vf[y * Z + i]
        for d in range(1, Y):
            total += h1[d, i].astype(F32)
        uf[i] = total
        ub[i] = total.astype(BF)
        return 0

    lax.fori_loop(0, Z, y_sum, 0)
    for d in range(1, Z):
        to = (z + d) % Z
        go(ub.at[to], h2.at[d], h2_s.at[d], h2_r.at[d], dev(zz=to))

    arrived(g3, g3_s.at[0], g3_r.at[0])
    total = line_sum(h) + g3[...].astype(F32)
    for k in range(4):
        tg_out[:, k * quarter:(k + 1) * quarter] = total[k * 8:k * 8 + 8].astype(BF)

    for d in range(1, Z):
        arrived(h2.at[d], h2_s.at[d], h2_r.at[d])
    total = uf[z]
    for d in range(1, Z):
        total += h2[d].astype(F32)
    for j in range(GROUP):
        wg_out[:, j * TILE:(j + 1) * TILE] = total * (my_pick == j).astype(F32)
    for op in sent:
        op.wait_send()


def make(mesh, dims):
    Y, Z, H, X = dims
    C = 2

    def per_device(tokens, weight, tile_pick, cotangent):
        D = tokens.shape[1]
        rows, cols = weight.shape
        group_rows = cotangent.shape[0]
        q = D // 4
        n = Y * Z
        dma = pltpu.SemaphoreType.DMA
        vm = pltpu.VMEM
        scratch = [
            vm((C * X * H, 32, q), BF), vm((n, rows, TILE), BF), vm((group_rows, D), BF),
            vm((group_rows, cols), F32), vm((group_rows, cols), BF), vm((group_rows, D), BF),
            vm((group_rows, D), F32),
            vm((X * H, 32, q), BF), vm((X * H, 32, q), BF), vm((X * H, 32, q), BF),
            vm((X, H, 32, q), BF), vm((32, q), BF), vm((32, q), BF),
            vm((n, rows, TILE), F32), vm((n, rows, TILE), BF), vm((Y, Z, rows, TILE), BF),
            vm((Z, rows, TILE), F32), vm((Z, rows, TILE), BF), vm((Z, rows, TILE), BF),
            dma((1,)), dma((1,)), dma((2, X)), dma((2, X)), dma((2, X)), dma((2, X)),
            dma((Z,)), dma((Z,)), dma((Y,)), dma((Y,)),
            dma((1,)), dma((1,)), dma((X,)), dma((X,)), dma((1,)), dma((1,)),
            dma((Y,)), dma((Y,)), dma((Z,)), dma((Z,)),
        ]
        spec = pl.BlockSpec(memory_space=pltpu.VMEM)
        return pl.pallas_call(
            functools.partial(kernel, dims),
            out_shape=(
                jax.ShapeDtypeStruct((group_rows, cols), BF),
                jax.ShapeDtypeStruct(tokens.shape, BF),
                jax.ShapeDtypeStruct((rows, cols), F32),
            ),
            in_specs=[spec, spec, pl.BlockSpec(memory_space=pltpu.SMEM), spec],
            out_specs=(spec, spec, spec),
            scratch_shapes=scratch,
            compiler_params=pltpu.CompilerParams(
                collective_id=0, has_side_effects=True, vmem_limit_bytes=40 * 2**20),
        )(tokens, weight, tile_pick, cotangent)

    placed = (P(("fsdp", "tensor"), None), P("fsdp", "tensor"), P(), P("fsdp", "tensor"))
    return jax.shard_map(
        per_device,
        mesh=mesh,
        in_specs=placed,
        out_specs=(P("fsdp", "tensor"), P(("fsdp", "tensor"), None), P("fsdp", "tensor")),
        check_vma=False,
    )


def solution(mesh):
    return make(mesh, (8, 8, 2, 4))
```

```python
import functools

import jax
import jax.numpy as jnp
from jax import lax
from jax.experimental import pallas as pl
from jax.experimental.pallas import tpu as pltpu
from jax.sharding import PartitionSpec as P

TILE = 128
GROUP = 7
BF = jnp.bfloat16
F32 = jnp.float32


def pair_order(p, k, pairs):
    if pairs != 4:
        return (p + k) % pairs
    inner = (p // 2 + p % 2) % 2
    kk = k if k < 2 else (2 + inner if k == 2 else 3 - inner)
    return (p // 2 + kk // 2) % 2 * 2 + (p % 2 + kk % 2) % 2


def kernel(dims, tok_hbm, w_hbm, picks, cot_hbm, act_out, tg_out, wg_out,
           tok_in, w_in, cot_in, tok, panel, xbuf, xt, acc, dpre, dpick, pf, pb, g1, sb, g2,
           rb, g3, vf, vb, h1, uf, ub, h2, in_s,
           t1_s, t1_r, t2_s, t2_r, t3_s, t3_r, w1_s, w1_r, w2_s, w2_r,
           g1_s, g1_r, g2_s, g2_r, g3_s, g3_r, h1_s, h1_r, h2_s, h2_r):
    Y, Z, H, X = dims
    C = 2
    NP = Z // 2
    rows = w_in.shape[0]
    D = tok_in.shape[1]
    quarter = D // 4
    tile_rows = D // TILE
    f = lax.axis_index("fsdp")
    t = lax.axis_index("tensor")
    y, z = f // Z, f % Z
    h, x, c = t // (X * C), (t // C) % X, t % C
    pz = z // 2

    def dev(yy=None, zz=None, hh=None, xx=None, cc=None):
        yy = y if yy is None else yy
        zz = z if zz is None else zz
        hh = h if hh is None else hh
        xx = x if xx is None else xx
        cc = c if cc is None else cc
        return (yy * Z + zz, (hh * X + xx) * C + cc)

    sibling = dev(cc=1 - c)
    partner = dev(hh=1 - h)
    peers = (
        [dev(zz=(z + d) % Z) for d in range(1, Z)]
        + [partner]
        + [dev(yy=(y + d) % Y) for d in range(1, Y)]
        + [dev(xx=(x + d) % X) for d in range(1, X)]
        + [sibling]
    )
    barrier = pltpu.get_barrier_semaphore()
    for p in peers:
        pl.semaphore_signal(barrier, inc=1, device_id=p, device_id_type=pl.DeviceIdType.MESH)

    loads = [pltpu.make_async_copy(a, b, in_s.at[i]) for i, (a, b) in enumerate(
        ((w_hbm, w_in), (tok_hbm, tok_in), (cot_hbm, cot_in)))]
    for op in loads:
        op.start()

    def copy(src, dst, ss, rs, device):
        return pltpu.make_async_remote_copy(
            src_ref=src, dst_ref=dst, send_sem=ss, recv_sem=rs,
            device_id=device, device_id_type=pl.DeviceIdType.MESH)

    sent = []

    def go(src, dst, ss, rs, device):
        op = copy(src, dst, ss, rs, device)
        op.start()
        sent.append(op)

    def arrived(dst, ss, rs):
        copy(dst, dst, ss, rs, sibling).wait_recv()

    def chosen(p, j):
        return jnp.full((1, TILE), (p == j).astype(F32)).astype(BF)

    def lanes(r):
        return pl.ds(pl.multiple_of(r * TILE, TILE), TILE)

    def piece(cc, xx, hh):
        return (cc * X + xx) * H + hh

    my_pick = picks[(f * rows) // TILE, t]
    loads[0].wait()
    mine = jnp.zeros((rows, TILE), BF)
    for j in range(GROUP):
        mine += w_in[:, j * TILE:(j + 1) * TILE] * chosen(my_pick, j)
    panel[f] = mine
    loads[1].wait()
    own = tok_in[...].astype(F32)
    own = jnp.concatenate([own[:, k * quarter:(k + 1) * quarter] for k in range(4)], axis=0)
    me = piece(c, x, h)
    tok[me] = own.astype(BF)

    def pair(k):
        return pair_order(pz, k, NP)

    def z_peer(n):
        if n == 0:
            return z + 1 - 2 * (z % 2)
        return pair((n + 1) // 2) * 2 + (n + 1) % 2

    def z_peers_of(k):
        return [0] if k == 0 else [2 * k - 1, 2 * k]

    pl.semaphore_wait(barrier, len(peers))

    go(tok.at[me], tok.at[me], t1_s.at[0], t1_r.at[0], partner)
    for n in range(Z - 1):
        go(panel.at[f], panel.at[f], w1_s.at[n], w1_r.at[z], dev(zz=z_peer(n)))
    for d in range(1, X):
        go(tok.at[me], tok.at[me], t2_s.at[0, d], t2_r.at[0, d], dev(xx=(x + d) % X))
    go(tok.at[me], tok.at[me], t3_s.at[0, 0], t3_r.at[0, 0], sibling)

    def weights_on(k):
        for n in z_peers_of(k):
            zs = z_peer(n)
            arrived(panel.at[y * Z + zs], w1_s.at[n], w1_r.at[zs])
        src = panel.at[pl.ds(y * Z + pair(k) * 2, 2)]
        for d in range(1, Y):
            go(src, src, w2_s.at[k, d], w2_r.at[k, d], dev(yy=(y + d) % Y))

    def tokens_on(rel):
        for d in range(1, X):
            src = piece(c, (x - d + X) % X, h if rel == 0 else 1 - h)
            arrived(tok.at[src], t2_s.at[rel, d], t2_r.at[rel, d])
            go(tok.at[src], tok.at[src], t3_s.at[rel, d], t3_r.at[rel, d], sibling)

    weights_on(0)
    if NP > 1:
        weights_on(1)
    tokens_on(0)
    for k in range(2, NP - 1):
        weights_on(k)
    src = piece(c, x, 1 - h)
    arrived(tok.at[src], t1_s.at[0], t1_r.at[0])
    for d in range(1, X):
        go(tok.at[src], tok.at[src], t2_s.at[1, d], t2_r.at[1, d], dev(xx=(x + d) % X))
    go(tok.at[src], tok.at[src], t3_s.at[1, 0], t3_r.at[1, 0], sibling)
    if NP > 2:
        weights_on(NP - 1)
    tokens_on(1)
    for k in range(2):
        for d in range(X):
            src = piece(1 - c, (x - d + X) % X, h if k == 0 else 1 - h)
            arrived(tok.at[src], t3_s.at[k, d], t3_r.at[k, d])

    def assemble(i, _):
        hh, xx = i // X, i % X
        a = tok[piece(0, xx, hh)].astype(F32)
        b = tok[piece(1, xx, hh)].astype(F32)
        at = pl.ds(pl.multiple_of(i * 16, 16), 16)
        for k in range(4):
            both = jnp.concatenate([a[k * 8:k * 8 + 8], b[k * 8:k * 8 + 8]], axis=0)
            xbuf[at, k * quarter:(k + 1) * quarter] = both.astype(BF)
        return 0

    lax.fori_loop(0, H * X, assemble, 0, unroll=2)

    def transpose(r, _):
        xt[r] = xbuf[:, lanes(r)].T
        return 0

    lax.fori_loop(0, tile_rows, transpose, 0, unroll=4)

    def tile_of(r):
        return panel[pl.ds(r * 2, 2)].reshape(TILE, TILE)

    for k in range(NP):
        for d in range(1, Y):
            at = pl.ds((y - d + Y) % Y * Z + pair(k) * 2, 2)
            arrived(panel.at[at], w2_s.at[k, d], w2_r.at[k, d])
        left, wide = [], []
        for yy in range(Y):
            r = yy * NP + pair(k)
            p = picks[r, t]
            w = tile_of(r)
            left.append(xbuf[:, lanes(r)])
            wide.append(jnp.concatenate([w * chosen(p, j) for j in range(GROUP)], axis=1))
        part = jnp.dot(jnp.concatenate(left, axis=1), jnp.concatenate(wide, axis=0),
                       preferred_element_type=F32)
        if k == 0:
            acc[...] = part
        else:
            acc[...] += part
    loads[2].wait()
    for j in range(GROUP):
        at = slice(j * TILE, (j + 1) * TILE)
        pre = acc[:, at]
        s = jax.nn.sigmoid(pre)
        act_out[:, at] = (pre * s).astype(BF)
        dpre[:, at] = (cot_in[:, at].astype(F32) * s * (1.0 + pre * (1.0 - s))).astype(BF)

    def weight_part(k, yy):
        r = yy * NP + pair(k)
        p = picks[r, t]
        total = dpre[:, 0:TILE] * chosen(p, 0)
        for j in range(1, GROUP):
            total += dpre[:, j * TILE:(j + 1) * TILE] * chosen(p, j)
        dpick[:, lanes(r)] = total
        g = jnp.dot(xt[r], total, preferred_element_type=F32)
        vb[r] = g.astype(BF)
        vf[r] = g

    for k in reversed(range(NP)):
        for yy in range(Y):
            weight_part(k, yy)
        for d in range(1, Y):
            to = (y + d) % Y
            go(vb.at[to * NP + pair(k)], h1.at[k, d], h1_s.at[k, d], h1_r.at[k, d], dev(yy=to))

    def token_part(r, _):
        pf[:, lanes(r)] = lax.dot_general(dpick[:, lanes(r)], tile_of(r), (((1,), (1,)), ((), ())),
                                          preferred_element_type=F32)
        return 0

    lax.fori_loop(0, tile_rows, token_part, 0, unroll=min(8, tile_rows))

    def row_piece(cc, xx, hh):
        at = pl.ds(pl.multiple_of(((hh * X + xx) * C + cc) * 8, 8), 8)
        return jnp.concatenate(
            [pf[at, k * quarter:(k + 1) * quarter] for k in range(4)], axis=0)

    h_of = (1 - h, h)
    for rel in range(2):
        for xx in range(X):
            pb[rel, xx] = row_piece(1 - c, xx, h_of[rel]).astype(BF)
        go(pb.at[rel], g1.at[rel], g1_s.at[rel], g1_r.at[rel], sibling)
    for rel in range(2):
        arrived(g1.at[rel], g1_s.at[rel], g1_r.at[rel])
        for d in range(1, X):
            to = (x + d) % X
            sb[rel, d] = (row_piece(c, to, h_of[rel]) + g1[rel, to].astype(F32)).astype(BF)
            go(sb.at[rel, d], g2.at[rel, d], g2_s.at[rel, d], g2_r.at[rel, d], dev(xx=to))

    def line_sum(rel):
        total = row_piece(c, x, h_of[rel]) + g1[rel, x].astype(F32)
        for d in range(1, X):
            arrived(g2.at[rel, d], g2_s.at[rel, d], g2_r.at[rel, d])
            total += g2[rel, d].astype(F32)
        return total

    rb[...] = line_sum(0).astype(BF)
    go(rb, g3, g3_s.at[0], g3_r.at[0], partner)
    own_tokens = line_sum(1)

    for k in reversed(range(NP)):
        total = vf[y * NP + pair(k)]
        for d in range(1, Y):
            arrived(h1.at[k, d], h1_s.at[k, d], h1_r.at[k, d])
            total += h1[k, d].astype(F32)
        total = total.reshape(2, rows, TILE)
        ub[k] = total.astype(BF)
        if k == 0:
            uf[...] = total
        for n in z_peers_of(k):
            to = z_peer(n)
            go(ub.at[k, to % 2], h2.at[z], h2_s.at[n], h2_r.at[z], dev(zz=to))

    arrived(g3, g3_s.at[0], g3_r.at[0])
    total = own_tokens + g3[...].astype(F32)
    for k in range(4):
        tg_out[:, k * quarter:(k + 1) * quarter] = total[k * 8:k * 8 + 8].astype(BF)

    total = uf[z % 2]
    for n in reversed(range(Z - 1)):
        zs = z_peer(n)
        arrived(h2.at[zs], h2_s.at[n], h2_r.at[zs])
        total += h2[zs].astype(F32)
    for j in range(GROUP):
        wg_out[:, j * TILE:(j + 1) * TILE] = total * (my_pick == j).astype(F32)
    for op in sent:
        op.wait_send()


def make(mesh, dims):
    Y, Z, H, X = dims
    C = 2
    NP = Z // 2

    def per_device(tokens, weight, tile_pick, cotangent):
        D = tokens.shape[1]
        rows, cols = weight.shape
        group_rows = cotangent.shape[0]
        q = D // 4
        n = Y * Z
        tr = D // TILE
        dma = pltpu.SemaphoreType.DMA
        vm = pltpu.VMEM
        scratch = [
            vm(tokens.shape, BF), vm(weight.shape, BF), vm(cotangent.shape, BF),
            vm((C * X * H, 32, q), BF), vm((n, rows, TILE), BF), vm((group_rows, D), BF),
            vm((tr, TILE, group_rows), BF),
            vm((group_rows, cols), F32), vm((group_rows, cols), BF), vm((group_rows, D), BF),
            vm((group_rows, D), F32),
            vm((H, X, 32, q), BF), vm((H, X, 32, q), BF), vm((H, X, 32, q), BF),
            vm((H, X, 32, q), BF), vm((32, q), BF), vm((32, q), BF),
            vm((tr, TILE, TILE), F32), vm((tr, TILE, TILE), BF), vm((NP, Y, TILE, TILE), BF),
            vm((2, rows, TILE), F32), vm((NP, 2, rows, TILE), BF), vm((Z, rows, TILE), BF),
            dma((3,)),
            dma((1,)), dma((1,)), dma((2, X)), dma((2, X)), dma((2, X)), dma((2, X)),
            dma((Z,)), dma((Z,)), dma((NP, Y)), dma((NP, Y)),
            dma((2,)), dma((2,)), dma((2, X)), dma((2, X)), dma((1,)), dma((1,)),
            dma((NP, Y)), dma((NP, Y)), dma((Z,)), dma((Z,)),
        ]
        spec = pl.BlockSpec(memory_space=pltpu.VMEM)
        far = pl.BlockSpec(memory_space=pltpu.HBM)
        return pl.pallas_call(
            functools.partial(kernel, dims),
            out_shape=(
                jax.ShapeDtypeStruct((group_rows, cols), BF),
                jax.ShapeDtypeStruct(tokens.shape, BF),
                jax.ShapeDtypeStruct((rows, cols), F32),
            ),
            in_specs=[far, far, pl.BlockSpec(memory_space=pltpu.SMEM), far],
            out_specs=(spec, spec, spec),
            scratch_shapes=scratch,
            compiler_params=pltpu.CompilerParams(
                collective_id=0, has_side_effects=True, vmem_limit_bytes=40 * 2**20),
        )(tokens, weight, tile_pick, cotangent)

    placed = (P(("fsdp", "tensor"), None), P("fsdp", "tensor"), P(), P("fsdp", "tensor"))
    return jax.shard_map(
        per_device,
        mesh=mesh,
        in_specs=placed,
        out_specs=(P("fsdp", "tensor"), P(("fsdp", "tensor"), None), P("fsdp", "tensor")),
        check_vma=False,
    )


def solution(mesh):
    return make(mesh, (8, 8, 2, 4))
```

```python
import functools

import jax
import jax.numpy as jnp
from jax import lax
from jax.experimental import pallas as pl
from jax.experimental.pallas import tpu as pltpu
from jax.sharding import PartitionSpec as P

TILE = 128
GROUP = 7
BF = jnp.bfloat16
F32 = jnp.float32
GRANT = 40 * 2**20


def pair_order(p, k, pairs):
    if pairs != 4:
        return (p + k) % pairs
    inner = (p // 2 + p % 2) % 2
    kk = k if k < 2 else (2 + inner if k == 2 else 3 - inner)
    return (p // 2 + kk // 2) % 2 * 2 + (p % 2 + kk % 2) % 2


def kernel(dims, tok_hbm, w_hbm, picks, cot_hbm, act_out, tg_out, wg_out,
           tok_in, w_in, cot_in, tok, panel, xbuf, xt, acc, dpre, dpick, pf, pb, g1, sb, g2,
           rb, g3, vf, hs, hr, uf, ub, h2, in_s,
           t1_s, t1_r, t2_s, t2_r, t3_s, t3_r, w1_s, w1_r, w2_s, w2_r,
           g1_s, g1_r, g2_s, g2_r, g3_s, g3_r, h1_s, h1_r, h2_s, h2_r):
    Y, Z, H, X = dims
    C = 2
    NP = Z // 2
    rows = w_in.shape[0]
    D = tok_in.shape[1]
    quarter = D // 4
    tile_rows = D // TILE
    f = lax.axis_index("fsdp")
    t = lax.axis_index("tensor")
    y, z = f // Z, f % Z
    h, x, c = t // (X * C), (t // C) % X, t % C
    pz = z // 2

    def dev(yy=None, zz=None, hh=None, xx=None, cc=None):
        yy = y if yy is None else yy
        zz = z if zz is None else zz
        hh = h if hh is None else hh
        xx = x if xx is None else xx
        cc = c if cc is None else cc
        return (yy * Z + zz, (hh * X + xx) * C + cc)

    sibling = dev(cc=1 - c)
    partner = dev(hh=1 - h)
    right, left = dev(yy=(y + 1) % Y), dev(yy=(y + Y - 1) % Y)
    peers = (
        [dev(zz=(z + d) % Z) for d in range(1, Z)]
        + [partner]
        + [right, left]
        + [dev(xx=(x + d) % X) for d in range(1, X)]
        + [sibling]
    )
    barrier = pltpu.get_barrier_semaphore()
    for p in peers:
        pl.semaphore_signal(barrier, inc=1, device_id=p, device_id_type=pl.DeviceIdType.MESH)

    loads = [pltpu.make_async_copy(a, b, in_s.at[i]) for i, (a, b) in enumerate(
        ((w_hbm, w_in), (tok_hbm, tok_in), (cot_hbm, cot_in)))]
    for op in loads:
        op.start()

    def copy(src, dst, ss, rs, device):
        return pltpu.make_async_remote_copy(
            src_ref=src, dst_ref=dst, send_sem=ss, recv_sem=rs,
            device_id=device, device_id_type=pl.DeviceIdType.MESH)

    sent = []

    def go(src, dst, ss, rs, device):
        op = copy(src, dst, ss, rs, device)
        op.start()
        sent.append(op)

    def arrived(dst, ss, rs):
        copy(dst, dst, ss, rs, sibling).wait_recv()

    def chosen(p, j):
        return jnp.full((1, TILE), (p == j).astype(F32)).astype(BF)

    def lanes(r):
        return pl.ds(pl.multiple_of(r * TILE, TILE), TILE)

    def piece(cc, xx, hh):
        return (cc * X + xx) * H + hh

    my_pick = picks[t, (f * rows) // TILE]
    loads[0].wait()
    mine = jnp.zeros((rows, TILE), BF)
    for j in range(GROUP):
        mine += w_in[:, j * TILE:(j + 1) * TILE] * chosen(my_pick, j)
    panel[f] = mine
    loads[1].wait()
    own = tok_in[...].astype(F32)
    own = jnp.concatenate([own[:, k * quarter:(k + 1) * quarter] for k in range(4)], axis=0)
    me = piece(c, x, h)
    tok[me] = own.astype(BF)

    def pair(k):
        return pair_order(pz, k, NP)

    def z_peer(n):
        if n == 0:
            return z + 1 - 2 * (z % 2)
        return pair((n + 1) // 2) * 2 + (n + 1) % 2

    def z_peers_of(k):
        return [0] if k == 0 else [2 * k - 1, 2 * k]

    pl.semaphore_wait(barrier, len(peers))

    go(tok.at[me], tok.at[me], t1_s.at[0], t1_r.at[0], partner)
    for n in range(Z - 1):
        go(panel.at[f], panel.at[f], w1_s.at[n], w1_r.at[z], dev(zz=z_peer(n)))
    for d in range(1, X):
        go(tok.at[me], tok.at[me], t2_s.at[0, d], t2_r.at[0, d], dev(xx=(x + d) % X))
    go(tok.at[me], tok.at[me], t3_s.at[0, 0], t3_r.at[0, 0], sibling)

    def hops(k, way):
        return Y // 2 if (k + way) % 2 == 0 else Y - 1 - Y // 2

    def behind(way, n):
        return (y - n + Y) % Y if way == 0 else (y + n) % Y

    def weights_go(k, way, hop):
        if hop < hops(k, way):
            at = panel.at[pl.ds(behind(way, hop) * Z + pair(k) * 2, 2)]
            go(at, at, w2_s.at[way, k, hop], w2_r.at[way, k, hop], left if way else right)

    def weights_here(k, way, hop):
        at = panel.at[pl.ds(behind(way, hop + 1) * Z + pair(k) * 2, 2)]
        arrived(at, w2_s.at[way, k, hop], w2_r.at[way, k, hop])

    def weights_start(k):
        for n in z_peers_of(k):
            zs = z_peer(n)
            arrived(panel.at[y * Z + zs], w1_s.at[n], w1_r.at[zs])
        for way in range(2):
            weights_go(k, way, 0)

    def weights_on(k, way, hop):
        weights_here(k, way, hop)
        weights_go(k, way, hop + 1)

    def tokens_on(rel):
        for d in range(1, X):
            src = piece(c, (x - d + X) % X, h if rel == 0 else 1 - h)
            arrived(tok.at[src], t2_s.at[rel, d], t2_r.at[rel, d])
            go(tok.at[src], tok.at[src], t3_s.at[rel, d], t3_r.at[rel, d], sibling)

    def partner_on():
        src = piece(c, x, 1 - h)
        arrived(tok.at[src], t1_s.at[0], t1_r.at[0])
        for d in range(1, X):
            go(tok.at[src], tok.at[src], t2_s.at[1, d], t2_r.at[1, d], dev(xx=(x + d) % X))
        go(tok.at[src], tok.at[src], t3_s.at[1, 0], t3_r.at[1, 0], sibling)

    steps = [(4.0, 0, tokens_on, (0,)), (8.0, 1, partner_on, ()), (11.0, 2, tokens_on, (1,))]
    for k in range(NP):
        start = 6.5 if k == NP - 1 else 5.0
        steps.append((start, 3 + k, weights_start, (k,)))
        for way in range(2):
            for hop in range(hops(k, way) - 1):
                steps.append((start + 2.6 * (hop + 1), 3 + k, weights_on, (k, way, hop)))
    for _, _, step, what in sorted(steps, key=lambda s: (s[0], s[1], s[3])):
        step(*what)
    for k in range(2):
        for d in range(X):
            src = piece(1 - c, (x - d + X) % X, h if k == 0 else 1 - h)
            arrived(tok.at[src], t3_s.at[k, d], t3_r.at[k, d])

    def assemble(i, _):
        hh, xx = i // X, i % X
        a = tok[piece(0, xx, hh)].astype(F32)
        b = tok[piece(1, xx, hh)].astype(F32)
        at = pl.ds(pl.multiple_of(i * 16, 16), 16)
        for k in range(4):
            both = jnp.concatenate([a[k * 8:k * 8 + 8], b[k * 8:k * 8 + 8]], axis=0)
            xbuf[at, k * quarter:(k + 1) * quarter] = both.astype(BF)
        return 0

    lax.fori_loop(0, H * X, assemble, 0, unroll=2)

    def transpose(r, _):
        xt[r] = xbuf[:, lanes(r)].T
        return 0

    lax.fori_loop(0, tile_rows, transpose, 0, unroll=4)

    def tile_of(r):
        return panel[pl.ds(r * 2, 2)].reshape(TILE, TILE)

    for k in range(NP):
        for way in range(2):
            if hops(k, way):
                weights_here(k, way, hops(k, way) - 1)
        across, wide = [], []
        for yy in range(Y):
            r = yy * NP + pair(k)
            p = picks[t, r]
            w = tile_of(r)
            across.append(xbuf[:, lanes(r)])
            wide.append(jnp.concatenate([w * chosen(p, j) for j in range(GROUP)], axis=1))
        part = jnp.dot(jnp.concatenate(across, axis=1), jnp.concatenate(wide, axis=0),
                       preferred_element_type=F32)
        if k == 0:
            acc[...] = part
        else:
            acc[...] += part
    loads[2].wait()
    for j in range(GROUP):
        at = slice(j * TILE, (j + 1) * TILE)
        pre = acc[:, at]
        s = jax.nn.sigmoid(pre)
        act_out[:, at] = (pre * s).astype(BF)
        dpre[:, at] = (cot_in[:, at].astype(F32) * s * (1.0 + pre * (1.0 - s))).astype(BF)

    def weight_part(k, yy):
        r = yy * NP + pair(k)
        p = picks[t, r]
        total = dpre[:, 0:TILE] * chosen(p, 0)
        for j in range(1, GROUP):
            total += dpre[:, j * TILE:(j + 1) * TILE] * chosen(p, j)
        dpick[:, lanes(r)] = total
        g = jnp.dot(xt[r], total, preferred_element_type=F32)
        vf[r] = g
        return g

    def sums_go(k, way, hop, value):
        hs[way, k, hop] = value.astype(BF)
        go(hs.at[way, k, hop], hr.at[way, k, hop], h1_s.at[way, k, hop], h1_r.at[way, k, hop],
           left if way else right)

    def sums_here(k, way, hop):
        arrived(hr.at[way, k, hop], h1_s.at[way, k, hop], h1_r.at[way, k, hop])
        return hr[way, k, hop].astype(F32)

    def sums_on(k, hop):
        for way in range(2):
            if hop + 1 < hops(k, way):
                to = behind(1 - way, hops(k, way) - 1 - hop)
                sums_go(k, way, hop + 1, sums_here(k, way, hop) + vf[to * NP + pair(k)])

    for k in reversed(range(NP)):
        for way in range(2):
            if hops(k, way):
                sums_go(k, way, 0, weight_part(k, behind(1 - way, hops(k, way))))
    for k in reversed(range(NP)):
        done = {hops(k, 0) or Y, Y - hops(k, 1)}
        for off in range(Y):
            if (off or Y) not in done or off == 0:
                weight_part(k, (y + off) % Y)

    def token_part(r, _):
        pf[:, lanes(r)] = lax.dot_general(dpick[:, lanes(r)], tile_of(r), (((1,), (1,)), ((), ())),
                                          preferred_element_type=F32)
        return 0

    lax.fori_loop(0, tile_rows, token_part, 0, unroll=min(8, tile_rows))

    def row_piece(cc, xx, hh):
        at = pl.ds(pl.multiple_of(((hh * X + xx) * C + cc) * 8, 8), 8)
        return jnp.concatenate(
            [pf[at, k * quarter:(k + 1) * quarter] for k in range(4)], axis=0)

    h_of = (1 - h, h)
    for rel in range(2):
        for xx in range(X):
            pb[rel, xx] = row_piece(1 - c, xx, h_of[rel]).astype(BF)
        go(pb.at[rel], g1.at[rel], g1_s.at[rel], g1_r.at[rel], sibling)
    for k in reversed(range(NP)):
        sums_on(k, 0)
    for rel in range(2):
        arrived(g1.at[rel], g1_s.at[rel], g1_r.at[rel])
        for d in range(1, X):
            to = (x + d) % X
            sb[rel, d] = (row_piece(c, to, h_of[rel]) + g1[rel, to].astype(F32)).astype(BF)
            go(sb.at[rel, d], g2.at[rel, d], g2_s.at[rel, d], g2_r.at[rel, d], dev(xx=to))

    def line_sum(rel):
        total = row_piece(c, x, h_of[rel]) + g1[rel, x].astype(F32)
        for d in range(1, X):
            arrived(g2.at[rel, d], g2_s.at[rel, d], g2_r.at[rel, d])
            total += g2[rel, d].astype(F32)
        return total

    for k in reversed(range(NP)):
        sums_on(k, 1)
    rb[...] = line_sum(0).astype(BF)
    go(rb, g3, g3_s.at[0], g3_r.at[0], partner)
    for hop in range(2, Y // 2):
        for k in reversed(range(NP)):
            sums_on(k, hop)
    own_tokens = line_sum(1)

    for k in reversed(range(NP)):
        total = vf[y * NP + pair(k)]
        for way in range(2):
            if hops(k, way):
                total += sums_here(k, way, hops(k, way) - 1)
        total = total.reshape(2, rows, TILE)
        ub[k] = total.astype(BF)
        if k == 0:
            uf[...] = total
        for n in z_peers_of(k):
            to = z_peer(n)
            go(ub.at[k, to % 2], h2.at[z], h2_s.at[n], h2_r.at[z], dev(zz=to))

    arrived(g3, g3_s.at[0], g3_r.at[0])
    total = own_tokens + g3[...].astype(F32)
    for k in range(4):
        tg_out[:, k * quarter:(k + 1) * quarter] = total[k * 8:k * 8 + 8].astype(BF)

    total = uf[z % 2]
    for n in reversed(range(Z - 1)):
        zs = z_peer(n)
        arrived(h2.at[zs], h2_s.at[n], h2_r.at[zs])
        total += h2[zs].astype(F32)
    for j in range(GROUP):
        wg_out[:, j * TILE:(j + 1) * TILE] = total * (my_pick == j).astype(F32)
    for op in sent:
        op.wait_send()


def write_out(a, b, c, a_out, b_out, c_out, sems):
    ops = [pltpu.make_async_copy(src, dst, sems.at[i])
           for i, (src, dst) in enumerate(((a, a_out), (b, b_out), (c, c_out)))]
    for op in ops:
        op.start()
    for op in ops:
        op.wait()


def make(mesh, dims):
    Y, Z, H, X = dims
    C = 2
    NP = Z // 2

    def per_device(tokens, weight, tile_pick, cotangent):
        D = tokens.shape[1]
        rows, cols = weight.shape
        group_rows = cotangent.shape[0]
        q = D // 4
        n = Y * Z
        tr = D // TILE
        dma = pltpu.SemaphoreType.DMA
        vm = pltpu.VMEM
        scratch = [
            vm(tokens.shape, BF), vm(weight.shape, BF), vm(cotangent.shape, BF),
            vm((C * X * H, 32, q), BF), vm((n, rows, TILE), BF), vm((group_rows, D), BF),
            vm((tr, TILE, group_rows), BF),
            vm((group_rows, cols), F32), vm((group_rows, cols), BF), vm((group_rows, D), BF),
            vm((group_rows, D), F32),
            vm((H, X, 32, q), BF), vm((H, X, 32, q), BF), vm((H, X, 32, q), BF),
            vm((H, X, 32, q), BF), vm((32, q), BF), vm((32, q), BF),
            vm((tr, TILE, TILE), F32), vm((2, NP, Y // 2, TILE, TILE), BF),
            vm((2, NP, Y // 2, TILE, TILE), BF),
            vm((2, rows, TILE), F32), vm((NP, 2, rows, TILE), BF), vm((Z, rows, TILE), BF),
            dma((3,)),
            dma((1,)), dma((1,)), dma((2, X)), dma((2, X)), dma((2, X)), dma((2, X)),
            dma((Z,)), dma((Z,)), dma((2, NP, Y // 2)), dma((2, NP, Y // 2)),
            dma((2,)), dma((2,)), dma((2, X)), dma((2, X)), dma((1,)), dma((1,)),
            dma((2, NP, Y // 2)), dma((2, NP, Y // 2)), dma((Z,)), dma((Z,)),
        ]
        spec = pl.BlockSpec(memory_space=pltpu.VMEM)
        far = pl.BlockSpec(memory_space=pltpu.HBM)
        results = pl.pallas_call(
            functools.partial(kernel, dims),
            out_shape=(
                jax.ShapeDtypeStruct((group_rows, cols), BF),
                jax.ShapeDtypeStruct(tokens.shape, BF),
                jax.ShapeDtypeStruct((rows, cols), F32),
            ),
            in_specs=[far, far, pl.BlockSpec(memory_space=pltpu.SMEM), far],
            out_specs=(spec, spec, spec),
            scratch_shapes=scratch,
            compiler_params=pltpu.CompilerParams(
                collective_id=0, has_side_effects=True, vmem_limit_bytes=GRANT),
        )(tokens, weight, tile_pick.T, cotangent)
        return pl.pallas_call(
            write_out,
            out_shape=tuple(jax.ShapeDtypeStruct(r.shape, r.dtype) for r in results),
            in_specs=[far] * 3,
            out_specs=(far,) * 3,
            scratch_shapes=[dma((3,))],
            compiler_params=pltpu.CompilerParams(vmem_limit_bytes=GRANT),
        )(*results)

    placed = (P(("fsdp", "tensor"), None), P("fsdp", "tensor"), P(), P("fsdp", "tensor"))
    return jax.shard_map(
        per_device,
        mesh=mesh,
        in_specs=placed,
        out_specs=(P("fsdp", "tensor"), P(("fsdp", "tensor"), None), P("fsdp", "tensor")),
        check_vma=False,
    )


def solution(mesh):
    return make(mesh, (8, 8, 2, 4))
```

```python
import functools

import jax
import jax.numpy as jnp
from jax import lax
from jax.experimental import pallas as pl
from jax.experimental.pallas import tpu as pltpu
from jax.sharding import PartitionSpec as P

TILE = 128
GROUP = 7
BF = jnp.bfloat16
F32 = jnp.float32
GRANT = 54 * 2**20


def pair_order(p, k, pairs):
    if pairs != 4:
        return (p + k) % pairs
    inner = (p // 2 + p % 2) % 2
    kk = k if k < 2 else (2 + inner if k == 2 else 3 - inner)
    return (p // 2 + kk // 2) % 2 * 2 + (p % 2 + kk % 2) % 2


def kernel(dims, tok_hbm, w_hbm, picks, cot_hbm, act_out, tg_out, wg_out,
           tok_in, w_in, cot_in, tok, panel, xbuf, xt, acc, dpre, dpick, pf, pb, g1, sb, g2,
           rb, g3, vf, hs, hr, uf, ub, h2, in_s,
           t1_s, t1_r, t2_s, t2_r, t3_s, t3_r, w1_s, w1_r, w2_s, w2_r,
           g1_s, g1_r, g2_s, g2_r, g3_s, g3_r, h1_s, h1_r, h2_s, h2_r):
    Y, Z, H, X = dims
    C = 2
    NP = Z // 2
    rows = w_in.shape[0]
    D = tok_in.shape[1]
    quarter = D // 4
    tile_rows = D // TILE
    f = lax.axis_index("fsdp")
    t = lax.axis_index("tensor")
    y, z = f // Z, f % Z
    h, x, c = t // (X * C), (t // C) % X, t % C
    pz = z // 2

    def dev(yy=None, zz=None, hh=None, xx=None, cc=None):
        yy = y if yy is None else yy
        zz = z if zz is None else zz
        hh = h if hh is None else hh
        xx = x if xx is None else xx
        cc = c if cc is None else cc
        return (yy * Z + zz, (hh * X + xx) * C + cc)

    sibling = dev(cc=1 - c)
    partner = dev(hh=1 - h)
    right, left = dev(yy=(y + 1) % Y), dev(yy=(y + Y - 1) % Y)
    peers = (
        [dev(zz=(z + d) % Z) for d in range(1, Z)]
        + [partner]
        + [right, left]
        + [dev(xx=(x + d) % X) for d in range(1, X)]
        + [sibling]
    )
    barrier = pltpu.get_barrier_semaphore()
    for p in peers:
        pl.semaphore_signal(barrier, inc=1, device_id=p, device_id_type=pl.DeviceIdType.MESH)

    loads = [pltpu.make_async_copy(a, b, in_s.at[i]) for i, (a, b) in enumerate(
        ((w_hbm, w_in), (tok_hbm, tok_in), (cot_hbm, cot_in)))]
    for op in loads:
        op.start()

    def copy(src, dst, ss, rs, device):
        return pltpu.make_async_remote_copy(
            src_ref=src, dst_ref=dst, send_sem=ss, recv_sem=rs,
            device_id=device, device_id_type=pl.DeviceIdType.MESH)

    sent = []

    def go(src, dst, ss, rs, device):
        op = copy(src, dst, ss, rs, device)
        op.start()
        sent.append(op)

    def arrived(dst, ss, rs):
        copy(dst, dst, ss, rs, sibling).wait_recv()

    def chosen(p, j):
        return jnp.full((1, TILE), (p == j).astype(F32)).astype(BF)

    def lanes(r):
        return pl.ds(pl.multiple_of(r * TILE, TILE), TILE)

    def piece(cc, xx, hh):
        return (cc * X + xx) * H + hh

    my_pick = picks[t, (f * rows) // TILE]
    loads[0].wait()
    mine = jnp.zeros((rows, TILE), BF)
    for j in range(GROUP):
        mine += w_in[:, j * TILE:(j + 1) * TILE] * chosen(my_pick, j)
    panel[f] = mine
    loads[1].wait()
    own = tok_in[...].astype(F32)
    own = jnp.concatenate([own[:, k * quarter:(k + 1) * quarter] for k in range(4)], axis=0)
    me = piece(c, x, h)
    tok[me] = own.astype(BF)

    def pair(k):
        return pair_order(pz, k, NP)

    def z_peer(n):
        if n == 0:
            return z + 1 - 2 * (z % 2)
        return pair((n + 1) // 2) * 2 + (n + 1) % 2

    def z_peers_of(k):
        return [0] if k == 0 else [2 * k - 1, 2 * k]

    pl.semaphore_wait(barrier, len(peers))

    go(tok.at[me], tok.at[me], t1_s.at[0], t1_r.at[0], partner)
    for n in range(Z - 1):
        go(panel.at[f], panel.at[f], w1_s.at[n], w1_r.at[z], dev(zz=z_peer(n)))
    for d in range(1, X):
        go(tok.at[me], tok.at[me], t2_s.at[0, d], t2_r.at[0, d], dev(xx=(x + d) % X))
    go(tok.at[me], tok.at[me], t3_s.at[0, 0], t3_r.at[0, 0], sibling)

    def hops(k, way):
        return Y // 2 if (k + way) % 2 == 0 else Y - 1 - Y // 2

    def behind(way, n):
        return (y - n + Y) % Y if way == 0 else (y + n) % Y

    def weights_go(k, way, hop):
        if hop < hops(k, way):
            at = panel.at[pl.ds(behind(way, hop) * Z + pair(k) * 2, 2)]
            go(at, at, w2_s.at[way, k, hop], w2_r.at[way, k, hop], left if way else right)

    def weights_here(k, way, hop):
        at = panel.at[pl.ds(behind(way, hop + 1) * Z + pair(k) * 2, 2)]
        arrived(at, w2_s.at[way, k, hop], w2_r.at[way, k, hop])

    def weights_start(k):
        for n in z_peers_of(k):
            zs = z_peer(n)
            arrived(panel.at[y * Z + zs], w1_s.at[n], w1_r.at[zs])
        for way in range(2):
            weights_go(k, way, 0)

    def weights_on(k, way, hop):
        weights_here(k, way, hop)
        weights_go(k, way, hop + 1)

    def tokens_on(rel):
        for d in range(1, X):
            src = piece(c, (x - d + X) % X, h if rel == 0 else 1 - h)
            arrived(tok.at[src], t2_s.at[rel, d], t2_r.at[rel, d])
            go(tok.at[src], tok.at[src], t3_s.at[rel, d], t3_r.at[rel, d], sibling)

    def partner_on():
        src = piece(c, x, 1 - h)
        arrived(tok.at[src], t1_s.at[0], t1_r.at[0])
        for d in range(1, X):
            go(tok.at[src], tok.at[src], t2_s.at[1, d], t2_r.at[1, d], dev(xx=(x + d) % X))
        go(tok.at[src], tok.at[src], t3_s.at[1, 0], t3_r.at[1, 0], sibling)

    steps = [(3.0, 0, tokens_on, (0,)), (4.9, 1, partner_on, ()), (7.0, 2, tokens_on, (1,))]
    for k in range(NP):
        start = 6.5 if k == NP - 1 else 5.0
        steps.append((start, 3 + k, weights_start, (k,)))
        for way in range(2):
            for hop in range(hops(k, way) - 1):
                steps.append((start + 2.6 * (hop + 1), 3 + k, weights_on, (k, way, hop)))
    for _, _, step, what in sorted(steps, key=lambda s: (s[0], s[1], s[3])):
        step(*what)
    for k in range(2):
        for d in range(X):
            src = piece(1 - c, (x - d + X) % X, h if k == 0 else 1 - h)
            arrived(tok.at[src], t3_s.at[k, d], t3_r.at[k, d])

    def assemble(i, _):
        hh, xx = i // X, i % X
        a = tok[piece(0, xx, hh)].astype(F32)
        b = tok[piece(1, xx, hh)].astype(F32)
        at = pl.ds(pl.multiple_of(i * 16, 16), 16)
        for k in range(4):
            both = jnp.concatenate([a[k * 8:k * 8 + 8], b[k * 8:k * 8 + 8]], axis=0)
            xbuf[at, k * quarter:(k + 1) * quarter] = both.astype(BF)
        return 0

    lax.fori_loop(0, H * X, assemble, 0, unroll=2)

    def transpose(r, _):
        xt[r] = xbuf[:, lanes(r)].T
        return 0

    lax.fori_loop(0, tile_rows, transpose, 0, unroll=4)

    def tile_of(r):
        return panel[pl.ds(r * 2, 2)].reshape(TILE, TILE)

    for k in range(NP):
        for way in range(2):
            if hops(k, way):
                weights_here(k, way, hops(k, way) - 1)
        across, wide = [], []
        for yy in range(Y):
            r = yy * NP + pair(k)
            p = picks[t, r]
            w = tile_of(r)
            across.append(xbuf[:, lanes(r)])
            wide.append(jnp.concatenate([w * chosen(p, j) for j in range(GROUP)], axis=1))
        part = jnp.dot(jnp.concatenate(across, axis=1), jnp.concatenate(wide, axis=0),
                       preferred_element_type=F32)
        if k == 0:
            acc[...] = part
        else:
            acc[...] += part
    loads[2].wait()
    for j in range(GROUP):
        at = slice(j * TILE, (j + 1) * TILE)
        pre = acc[:, at]
        s = jax.nn.sigmoid(pre)
        act_out[:, at] = (pre * s).astype(BF)
        dpre[:, at] = (cot_in[:, at].astype(F32) * s * (1.0 + pre * (1.0 - s))).astype(BF)

    def weight_part(k, yy):
        r = yy * NP + pair(k)
        p = picks[t, r]
        total = dpre[:, 0:TILE] * chosen(p, 0)
        for j in range(1, GROUP):
            total += dpre[:, j * TILE:(j + 1) * TILE] * chosen(p, j)
        dpick[:, lanes(r)] = total
        g = jnp.dot(xt[r], total, preferred_element_type=F32)
        vf[r] = g
        return g

    def sums_go(k, way, hop, value):
        hs[way, k, hop] = value.astype(BF)
        go(hs.at[way, k, hop], hr.at[way, k, hop], h1_s.at[way, k, hop], h1_r.at[way, k, hop],
           left if way else right)

    def sums_here(k, way, hop):
        arrived(hr.at[way, k, hop], h1_s.at[way, k, hop], h1_r.at[way, k, hop])
        return hr[way, k, hop].astype(F32)

    def sums_on(k, hop):
        for way in range(2):
            if hop + 1 < hops(k, way):
                to = behind(1 - way, hops(k, way) - 1 - hop)
                sums_go(k, way, hop + 1, sums_here(k, way, hop) + vf[to * NP + pair(k)])

    for k in reversed(range(NP)):
        for way in range(2):
            if hops(k, way):
                sums_go(k, way, 0, weight_part(k, behind(1 - way, hops(k, way))))
    for k in reversed(range(NP)):
        done = {hops(k, 0) or Y, Y - hops(k, 1)}
        for off in range(Y):
            if (off or Y) not in done or off == 0:
                weight_part(k, (y + off) % Y)

    def token_part(r, _):
        pf[:, lanes(r)] = lax.dot_general(dpick[:, lanes(r)], tile_of(r), (((1,), (1,)), ((), ())),
                                          preferred_element_type=F32)
        return 0

    lax.fori_loop(0, tile_rows, token_part, 0, unroll=min(8, tile_rows))

    def row_piece(cc, xx, hh):
        at = pl.ds(pl.multiple_of(((hh * X + xx) * C + cc) * 8, 8), 8)
        return jnp.concatenate(
            [pf[at, k * quarter:(k + 1) * quarter] for k in range(4)], axis=0)

    h_of = (1 - h, h)
    for rel in range(2):
        for xx in range(X):
            pb[rel, xx] = row_piece(1 - c, xx, h_of[rel]).astype(BF)
        go(pb.at[rel], g1.at[rel], g1_s.at[rel], g1_r.at[rel], sibling)
    for k in reversed(range(NP)):
        sums_on(k, 0)
    for rel in range(2):
        arrived(g1.at[rel], g1_s.at[rel], g1_r.at[rel])
        for d in range(1, X):
            to = (x + d) % X
            sb[rel, d] = (row_piece(c, to, h_of[rel]) + g1[rel, to].astype(F32)).astype(BF)
            go(sb.at[rel, d], g2.at[rel, d], g2_s.at[rel, d], g2_r.at[rel, d], dev(xx=to))

    def line_sum(rel):
        total = row_piece(c, x, h_of[rel]) + g1[rel, x].astype(F32)
        for d in range(1, X):
            arrived(g2.at[rel, d], g2_s.at[rel, d], g2_r.at[rel, d])
            total += g2[rel, d].astype(F32)
        return total

    for k in reversed(range(NP)):
        sums_on(k, 1)
    rb[...] = line_sum(0).astype(BF)
    go(rb, g3, g3_s.at[0], g3_r.at[0], partner)
    for hop in range(2, Y // 2):
        for k in reversed(range(NP)):
            sums_on(k, hop)
    own_tokens = line_sum(1)

    for k in reversed(range(NP)):
        total = vf[y * NP + pair(k)]
        for way in range(2):
            if hops(k, way):
                total += sums_here(k, way, hops(k, way) - 1)
        total = total.reshape(2, rows, TILE)
        ub[k] = total.astype(BF)
        if k == 0:
            uf[...] = total
        for n in z_peers_of(k):
            to = z_peer(n)
            go(ub.at[k, to % 2], h2.at[z], h2_s.at[n], h2_r.at[z], dev(zz=to))

    arrived(g3, g3_s.at[0], g3_r.at[0])
    total = own_tokens + g3[...].astype(F32)
    for k in range(4):
        tg_out[:, k * quarter:(k + 1) * quarter] = total[k * 8:k * 8 + 8].astype(BF)

    total = uf[z % 2]
    for n in reversed(range(Z - 1)):
        zs = z_peer(n)
        arrived(h2.at[zs], h2_s.at[n], h2_r.at[zs])
        total += h2[zs].astype(F32)
    for j in range(GROUP):
        wg_out[:, j * TILE:(j + 1) * TILE] = total * (my_pick == j).astype(F32)
    for op in sent:
        op.wait_send()


def write_out(a, b, c, a_out, b_out, c_out, a_on, b_on, c_on, sems):
    way = ((a, a_on, a_out), (b, b_on, b_out), (c, c_on, c_out))
    ops = [pltpu.make_async_copy(src, on, sems.at[i]) for i, (src, on, _) in enumerate(way)]
    outs = [pltpu.make_async_copy(on, dst, sems.at[3 + i]) for i, (_, on, dst) in enumerate(way)]
    for op in ops:
        op.start()
    for op, out in zip(ops, outs):
        op.wait()
        out.start()
    for out in outs:
        out.wait()


def make(mesh, dims):
    Y, Z, H, X = dims
    C = 2
    NP = Z // 2

    def per_device(tokens, weight, tile_pick, cotangent):
        D = tokens.shape[1]
        rows, cols = weight.shape
        group_rows = cotangent.shape[0]
        q = D // 4
        n = Y * Z
        tr = D // TILE
        dma = pltpu.SemaphoreType.DMA
        vm = pltpu.VMEM
        scratch = [
            vm(tokens.shape, BF), vm(weight.shape, BF), vm(cotangent.shape, BF),
            vm((C * X * H, 32, q), BF), vm((n, rows, TILE), BF), vm((group_rows, D), BF),
            vm((tr, TILE, group_rows), BF),
            vm((group_rows, cols), F32), vm((group_rows, cols), BF), vm((group_rows, D), BF),
            vm((group_rows, D), F32),
            vm((H, X, 32, q), BF), vm((H, X, 32, q), BF), vm((H, X, 32, q), BF),
            vm((H, X, 32, q), BF), vm((32, q), BF), vm((32, q), BF),
            vm((tr, TILE, TILE), F32), vm((2, NP, Y // 2, TILE, TILE), BF),
            vm((2, NP, Y // 2, TILE, TILE), BF),
            vm((2, rows, TILE), F32), vm((NP, 2, rows, TILE), BF), vm((Z, rows, TILE), BF),
            dma((3,)),
            dma((1,)), dma((1,)), dma((2, X)), dma((2, X)), dma((2, X)), dma((2, X)),
            dma((Z,)), dma((Z,)), dma((2, NP, Y // 2)), dma((2, NP, Y // 2)),
            dma((2,)), dma((2,)), dma((2, X)), dma((2, X)), dma((1,)), dma((1,)),
            dma((2, NP, Y // 2)), dma((2, NP, Y // 2)), dma((Z,)), dma((Z,)),
        ]
        spec = pl.BlockSpec(memory_space=pltpu.VMEM)
        far = pl.BlockSpec(memory_space=pltpu.HBM)
        results = pl.pallas_call(
            functools.partial(kernel, dims),
            out_shape=(
                jax.ShapeDtypeStruct((group_rows, cols), BF),
                jax.ShapeDtypeStruct(tokens.shape, BF),
                jax.ShapeDtypeStruct((rows, cols), F32),
            ),
            in_specs=[far, far, pl.BlockSpec(memory_space=pltpu.SMEM), far],
            out_specs=(spec, spec, spec),
            scratch_shapes=scratch,
            compiler_params=pltpu.CompilerParams(
                collective_id=0, has_side_effects=True, vmem_limit_bytes=GRANT),
        )(tokens, weight, tile_pick.T, cotangent)
        return pl.pallas_call(
            write_out,
            out_shape=tuple(jax.ShapeDtypeStruct(r.shape, r.dtype) for r in results),
            in_specs=[far] * 3,
            out_specs=(far,) * 3,
            scratch_shapes=[vm(r.shape, r.dtype) for r in results] + [dma((6,))],
            compiler_params=pltpu.CompilerParams(vmem_limit_bytes=GRANT),
        )(*results)

    placed = (P(("fsdp", "tensor"), None), P("fsdp", "tensor"), P(), P("fsdp", "tensor"))
    return jax.shard_map(
        per_device,
        mesh=mesh,
        in_specs=placed,
        out_specs=(P("fsdp", "tensor"), P(("fsdp", "tensor"), None), P("fsdp", "tensor")),
        check_vma=False,
    )


def solution(mesh):
    return make(mesh, (8, 8, 2, 4))
```

```python
import functools

import jax
import jax.numpy as jnp
from jax import lax
from jax.experimental import pallas as pl
from jax.experimental.pallas import tpu as pltpu
from jax.sharding import PartitionSpec as P

TILE = 128
GROUP = 7
BF = jnp.bfloat16
F32 = jnp.float32
GRANT = 54 * 2**20


def pair_order(p, k, pairs):
    if pairs != 4:
        return (p + k) % pairs
    inner = (p // 2 + p % 2) % 2
    kk = k if k < 2 else (2 + inner if k == 2 else 3 - inner)
    return (p // 2 + kk // 2) % 2 * 2 + (p % 2 + kk % 2) % 2


def kernel(dims, tok_hbm, w_hbm, picks, cot_hbm, act_out, tg_out, wg_out,
           tok_in, w_in, cot_in, tok, panel, xbuf, xt, acc, dpre, dpick, pf, pb, g1, sb, g2,
           rb, g3, vf, hs, hr, uf, ub, h2, in_s,
           t1_s, t1_r, t2_s, t2_r, t3_s, t3_r, w1_s, w1_r, w2_s, w2_r,
           g1_s, g1_r, g2_s, g2_r, g3_s, g3_r, h1_s, h1_r, h2_s, h2_r):
    Y, Z, H, X = dims
    C = 2
    NP = Z // 2
    rows = w_in.shape[0]
    D = tok_in.shape[1]
    quarter = D // 4
    tile_rows = D // TILE
    f = lax.axis_index("fsdp")
    t = lax.axis_index("tensor")
    y, z = f // Z, f % Z
    h, x, c = t // (X * C), (t // C) % X, t % C
    pz = z // 2

    def dev(yy=None, zz=None, hh=None, xx=None, cc=None):
        yy = y if yy is None else yy
        zz = z if zz is None else zz
        hh = h if hh is None else hh
        xx = x if xx is None else xx
        cc = c if cc is None else cc
        return (yy * Z + zz, (hh * X + xx) * C + cc)

    sibling = dev(cc=1 - c)
    partner = dev(hh=1 - h)
    right, left = dev(yy=(y + 1) % Y), dev(yy=(y + Y - 1) % Y)
    peers = (
        [dev(zz=(z + d) % Z) for d in range(1, Z)]
        + [partner]
        + [right, left]
        + [dev(xx=(x + d) % X) for d in range(1, X)]
        + [sibling]
    )
    barrier = pltpu.get_barrier_semaphore()
    for p in peers:
        pl.semaphore_signal(barrier, inc=1, device_id=p, device_id_type=pl.DeviceIdType.MESH)

    loads = [pltpu.make_async_copy(a, b, in_s.at[i]) for i, (a, b) in enumerate(
        ((w_hbm, w_in), (tok_hbm, tok_in), (cot_hbm, cot_in)))]
    for op in loads:
        op.start()

    def copy(src, dst, ss, rs, device):
        return pltpu.make_async_remote_copy(
            src_ref=src, dst_ref=dst, send_sem=ss, recv_sem=rs,
            device_id=device, device_id_type=pl.DeviceIdType.MESH)

    sent = []

    def go(src, dst, ss, rs, device):
        op = copy(src, dst, ss, rs, device)
        op.start()
        sent.append(op)

    def arrived(dst, ss, rs):
        copy(dst, dst, ss, rs, sibling).wait_recv()

    def chosen(p, j):
        return jnp.full((1, TILE), (p == j).astype(F32)).astype(BF)

    def lanes(r):
        return pl.ds(pl.multiple_of(r * TILE, TILE), TILE)

    def piece(cc, xx, hh):
        return (cc * X + xx) * H + hh

    my_pick = picks[t, (f * rows) // TILE]
    loads[0].wait()
    mine = jnp.zeros((rows, TILE), BF)
    for j in range(GROUP):
        mine += w_in[:, j * TILE:(j + 1) * TILE] * chosen(my_pick, j)
    panel[f] = mine
    loads[1].wait()
    own = tok_in[...].astype(F32)
    own = jnp.concatenate([own[:, k * quarter:(k + 1) * quarter] for k in range(4)], axis=0)
    me = piece(c, x, h)
    tok[me] = own.astype(BF)

    def pair(k):
        return pair_order(pz, k, NP)

    def z_peer(n):
        if n == 0:
            return z + 1 - 2 * (z % 2)
        return pair((n + 1) // 2) * 2 + (n + 1) % 2

    def z_peers_of(k):
        return [0] if k == 0 else [2 * k - 1, 2 * k]

    pl.semaphore_wait(barrier, len(peers))

    go(tok.at[me], tok.at[me], t1_s.at[0], t1_r.at[0], partner)
    for n in range(Z - 1):
        go(panel.at[f], panel.at[f], w1_s.at[n], w1_r.at[z], dev(zz=z_peer(n)))
    for d in range(1, X):
        go(tok.at[me], tok.at[me], t2_s.at[0, d], t2_r.at[0, d], dev(xx=(x + d) % X))
    go(tok.at[me], tok.at[me], t3_s.at[0, 0], t3_r.at[0, 0], sibling)

    def hops(k, way):
        return Y // 2 if (k + way) % 2 == 0 else Y - 1 - Y // 2

    def behind(way, n):
        return (y - n + Y) % Y if way == 0 else (y + n) % Y

    def weights_go(k, way, hop):
        if hop < hops(k, way):
            at = panel.at[pl.ds(behind(way, hop) * Z + pair(k) * 2, 2)]
            go(at, at, w2_s.at[way, k, hop], w2_r.at[way, k, hop], left if way else right)

    def weights_here(k, way, hop):
        at = panel.at[pl.ds(behind(way, hop + 1) * Z + pair(k) * 2, 2)]
        arrived(at, w2_s.at[way, k, hop], w2_r.at[way, k, hop])

    def weights_start(k):
        for n in z_peers_of(k):
            zs = z_peer(n)
            arrived(panel.at[y * Z + zs], w1_s.at[n], w1_r.at[zs])
        for way in range(2):
            weights_go(k, way, 0)

    def weights_on(k, way, hop):
        weights_here(k, way, hop)
        weights_go(k, way, hop + 1)

    def tokens_on(rel):
        for d in range(1, X):
            src = piece(c, (x - d + X) % X, h if rel == 0 else 1 - h)
            arrived(tok.at[src], t2_s.at[rel, d], t2_r.at[rel, d])
            go(tok.at[src], tok.at[src], t3_s.at[rel, d], t3_r.at[rel, d], sibling)

    def partner_on():
        src = piece(c, x, 1 - h)
        arrived(tok.at[src], t1_s.at[0], t1_r.at[0])
        for d in range(1, X):
            go(tok.at[src], tok.at[src], t2_s.at[1, d], t2_r.at[1, d], dev(xx=(x + d) % X))
        go(tok.at[src], tok.at[src], t3_s.at[1, 0], t3_r.at[1, 0], sibling)

    steps = [(3.0, 0, tokens_on, (0,)), (4.9, 1, partner_on, ()), (8.0, 2, tokens_on, (1,))]
    for k in range(NP):
        start = 6.5 if k == NP - 1 else 5.0
        steps.append((start, 3 + k, weights_start, (k,)))
        for way in range(2):
            for hop in range(hops(k, way) - 1):
                steps.append((start + 2.6 * (hop + 1), 3 + k, weights_on, (k, way, hop)))
    for _, _, step, what in sorted(steps, key=lambda s: (s[0], s[1], s[3])):
        step(*what)
    for k in range(2):
        for d in range(X):
            src = piece(1 - c, (x - d + X) % X, h if k == 0 else 1 - h)
            arrived(tok.at[src], t3_s.at[k, d], t3_r.at[k, d])

    def assemble(i, _):
        hh, xx = i // X, i % X
        a = tok[piece(0, xx, hh)].astype(F32)
        b = tok[piece(1, xx, hh)].astype(F32)
        at = pl.ds(pl.multiple_of(i * 16, 16), 16)
        for k in range(4):
            both = jnp.concatenate([a[k * 8:k * 8 + 8], b[k * 8:k * 8 + 8]], axis=0)
            xbuf[at, k * quarter:(k + 1) * quarter] = both.astype(BF)
        return 0

    lax.fori_loop(0, H * X, assemble, 0, unroll=2)

    def transpose(r, _):
        xt[r] = xbuf[:, lanes(r)].T
        return 0

    lax.fori_loop(0, tile_rows, transpose, 0, unroll=4)

    def tile_of(r):
        return panel[pl.ds(r * 2, 2)].reshape(TILE, TILE)

    for k in range(NP):
        for way in range(2):
            if hops(k, way):
                weights_here(k, way, hops(k, way) - 1)
        across, wide = [], []
        for yy in range(Y):
            r = yy * NP + pair(k)
            p = picks[t, r]
            w = tile_of(r)
            across.append(xbuf[:, lanes(r)])
            wide.append(jnp.concatenate([w * chosen(p, j) for j in range(GROUP)], axis=1))
        part = jnp.dot(jnp.concatenate(across, axis=1), jnp.concatenate(wide, axis=0),
                       preferred_element_type=F32)
        if k == 0:
            acc[...] = part
        else:
            acc[...] += part
    loads[2].wait()
    for j in range(GROUP):
        at = slice(j * TILE, (j + 1) * TILE)
        pre = acc[:, at]
        s = jax.nn.sigmoid(pre)
        act_out[:, at] = (pre * s).astype(BF)
        dpre[:, at] = (cot_in[:, at].astype(F32) * s * (1.0 + pre * (1.0 - s))).astype(BF)

    def weight_part(k, yy):
        r = yy * NP + pair(k)
        p = picks[t, r]
        total = dpre[:, 0:TILE] * chosen(p, 0)
        for j in range(1, GROUP):
            total += dpre[:, j * TILE:(j + 1) * TILE] * chosen(p, j)
        dpick[:, lanes(r)] = total
        g = jnp.dot(xt[r], total, preferred_element_type=F32)
        vf[r] = g
        return g

    def sums_go(k, way, hop, value):
        hs[way, k, hop] = value.astype(BF)
        go(hs.at[way, k, hop], hr.at[way, k, hop], h1_s.at[way, k, hop], h1_r.at[way, k, hop],
           left if way else right)

    def sums_here(k, way, hop):
        arrived(hr.at[way, k, hop], h1_s.at[way, k, hop], h1_r.at[way, k, hop])
        return hr[way, k, hop].astype(F32)

    def sums_on(k, hop):
        for way in range(2):
            if hop + 1 < hops(k, way):
                to = behind(1 - way, hops(k, way) - 1 - hop)
                sums_go(k, way, hop + 1, sums_here(k, way, hop) + vf[to * NP + pair(k)])

    for k in reversed(range(NP)):
        for way in range(2):
            if hops(k, way):
                sums_go(k, way, 0, weight_part(k, behind(1 - way, hops(k, way))))
    for k in reversed(range(NP)):
        done = {hops(k, 0) or Y, Y - hops(k, 1)}
        for off in range(Y):
            if (off or Y) not in done or off == 0:
                weight_part(k, (y + off) % Y)

    def token_part(r, _):
        pf[:, lanes(r)] = lax.dot_general(dpick[:, lanes(r)], tile_of(r), (((1,), (1,)), ((), ())),
                                          preferred_element_type=F32)
        return 0

    lax.fori_loop(0, tile_rows, token_part, 0, unroll=min(8, tile_rows))

    def row_piece(cc, xx, hh):
        at = pl.ds(pl.multiple_of(((hh * X + xx) * C + cc) * 8, 8), 8)
        return jnp.concatenate(
            [pf[at, k * quarter:(k + 1) * quarter] for k in range(4)], axis=0)

    h_of = (1 - h, h)
    for rel in range(2):
        for xx in range(X):
            pb[rel, xx] = row_piece(1 - c, xx, h_of[rel]).astype(BF)
        go(pb.at[rel], g1.at[rel], g1_s.at[rel], g1_r.at[rel], sibling)
    for k in reversed(range(NP)):
        sums_on(k, 0)
    for rel in range(2):
        arrived(g1.at[rel], g1_s.at[rel], g1_r.at[rel])
        for d in range(1, X):
            to = (x + d) % X
            sb[rel, d] = (row_piece(c, to, h_of[rel]) + g1[rel, to].astype(F32)).astype(BF)
            go(sb.at[rel, d], g2.at[rel, d], g2_s.at[rel, d], g2_r.at[rel, d], dev(xx=to))

    def line_sum(rel):
        total = row_piece(c, x, h_of[rel]) + g1[rel, x].astype(F32)
        for d in range(1, X):
            arrived(g2.at[rel, d], g2_s.at[rel, d], g2_r.at[rel, d])
            total += g2[rel, d].astype(F32)
        return total

    for k in reversed(range(NP)):
        sums_on(k, 1)
    rb[...] = line_sum(0).astype(BF)
    go(rb, g3, g3_s.at[0], g3_r.at[0], partner)
    for hop in range(2, Y // 2):
        for k in reversed(range(NP)):
            sums_on(k, hop)
    own_tokens = line_sum(1)

    for k in reversed(range(NP)):
        total = vf[y * NP + pair(k)]
        for way in range(2):
            if hops(k, way):
                total += sums_here(k, way, hops(k, way) - 1)
        total = total.reshape(2, rows, TILE)
        ub[k] = total.astype(BF)
        if k == 0:
            uf[...] = total
        for n in z_peers_of(k):
            to = z_peer(n)
            go(ub.at[k, to % 2], h2.at[z], h2_s.at[n], h2_r.at[z], dev(zz=to))

    arrived(g3, g3_s.at[0], g3_r.at[0])
    total = own_tokens + g3[...].astype(F32)
    for k in range(4):
        tg_out[:, k * quarter:(k + 1) * quarter] = total[k * 8:k * 8 + 8].astype(BF)

    total = uf[z % 2]
    for n in reversed(range(Z - 1)):
        zs = z_peer(n)
        arrived(h2.at[zs], h2_s.at[n], h2_r.at[zs])
        total += h2[zs].astype(F32)
    for j in range(GROUP):
        wg_out[:, j * TILE:(j + 1) * TILE] = total * (my_pick == j).astype(F32)
    for op in sent:
        op.wait_send()


def write_out(a, b, c, a_out, b_out, c_out, a_on, b_on, c_on, sems):
    way = ((a, a_on, a_out), (b, b_on, b_out), (c, c_on, c_out))
    ops = [pltpu.make_async_copy(src, on, sems.at[i]) for i, (src, on, _) in enumerate(way)]
    outs = [pltpu.make_async_copy(on, dst, sems.at[3 + i]) for i, (_, on, dst) in enumerate(way)]
    for op in ops:
        op.start()
    for op, out in zip(ops, outs):
        op.wait()
        out.start()
    for out in outs:
        out.wait()


def make(mesh, dims):
    Y, Z, H, X = dims
    C = 2
    NP = Z // 2

    def per_device(tokens, weight, tile_pick, cotangent):
        D = tokens.shape[1]
        rows, cols = weight.shape
        group_rows = cotangent.shape[0]
        q = D // 4
        n = Y * Z
        tr = D // TILE
        dma = pltpu.SemaphoreType.DMA
        vm = pltpu.VMEM
        scratch = [
            vm(tokens.shape, BF), vm(weight.shape, BF), vm(cotangent.shape, BF),
            vm((C * X * H, 32, q), BF), vm((n, rows, TILE), BF), vm((group_rows, D), BF),
            vm((tr, TILE, group_rows), BF),
            vm((group_rows, cols), F32), vm((group_rows, cols), BF), vm((group_rows, D), BF),
            vm((group_rows, D), F32),
            vm((H, X, 32, q), BF), vm((H, X, 32, q), BF), vm((H, X, 32, q), BF),
            vm((H, X, 32, q), BF), vm((32, q), BF), vm((32, q), BF),
            vm((tr, TILE, TILE), F32), vm((2, NP, Y // 2, TILE, TILE), BF),
            vm((2, NP, Y // 2, TILE, TILE), BF),
            vm((2, rows, TILE), F32), vm((NP, 2, rows, TILE), BF), vm((Z, rows, TILE), BF),
            dma((3,)),
            dma((1,)), dma((1,)), dma((2, X)), dma((2, X)), dma((2, X)), dma((2, X)),
            dma((Z,)), dma((Z,)), dma((2, NP, Y // 2)), dma((2, NP, Y // 2)),
            dma((2,)), dma((2,)), dma((2, X)), dma((2, X)), dma((1,)), dma((1,)),
            dma((2, NP, Y // 2)), dma((2, NP, Y // 2)), dma((Z,)), dma((Z,)),
        ]
        spec = pl.BlockSpec(memory_space=pltpu.VMEM)
        far = pl.BlockSpec(memory_space=pltpu.HBM)
        results = pl.pallas_call(
            functools.partial(kernel, dims),
            out_shape=(
                jax.ShapeDtypeStruct((group_rows, cols), BF),
                jax.ShapeDtypeStruct(tokens.shape, BF),
                jax.ShapeDtypeStruct((rows, cols), F32),
            ),
            in_specs=[far, far, pl.BlockSpec(memory_space=pltpu.SMEM), far],
            out_specs=(spec, spec, spec),
            scratch_shapes=scratch,
            compiler_params=pltpu.CompilerParams(
                collective_id=0, has_side_effects=True, vmem_limit_bytes=GRANT),
        )(tokens, weight, tile_pick.T, cotangent)
        return pl.pallas_call(
            write_out,
            out_shape=tuple(jax.ShapeDtypeStruct(r.shape, r.dtype) for r in results),
            in_specs=[far] * 3,
            out_specs=(far,) * 3,
            scratch_shapes=[vm(r.shape, r.dtype) for r in results] + [dma((6,))],
            compiler_params=pltpu.CompilerParams(vmem_limit_bytes=GRANT),
        )(*results)

    placed = (P(("fsdp", "tensor"), None), P("fsdp", "tensor"), P(), P("fsdp", "tensor"))
    return jax.shard_map(
        per_device,
        mesh=mesh,
        in_specs=placed,
        out_specs=(P("fsdp", "tensor"), P(("fsdp", "tensor"), None), P("fsdp", "tensor")),
        check_vma=False,
    )


def solution(mesh):
    return make(mesh, (8, 8, 2, 4))
```
